32 devices in a mesh: lon: 4 (over z), lat: 4 (over y, core), ch: 2 (over x).
Axes of the slice: x: 2, y: 2, z: 4, core: 2. Of those that a mesh axis runs over, the one named last changes fastest.
Arguments:
- state_field: bfloat16 [60, 720, 256], P('lat', 'lon', 'ch'), may hold values from -6 to 6
- cotangent: bfloat16 [60, 720, 256], P('lat', 'lon', 'ch'), may hold values from -6 to 6
- conv_kernel: float32 [2, 7, 7, 256], P(None, None, None, 'ch'), may hold values from -0.875 to 0.875
- conv_bias: float32 [2, 256], P(None, 'ch'), may hold values from -3 to 3
- norm_gain: float32 [2, 256], P(None, 'ch'), may hold values from 0.5 to 1.5
- weight_in: bfloat16 [2, 256, 1024], replicated, may hold values from -0.375 to 0.375
- bias_in: float32 [2, 1024], replicated, may hold values from -3 to 3
- weight_out: bfloat16 [2, 1024, 256], replicated, may hold values from -0.1875 to 0.1875
- layer_scale: float32 [2, 256], P(None, 'ch'), may hold values from 0.5 to 1.5
Outputs:
- gradient_field: float32 [60, 720, 256], P('lat', 'lon', 'ch')
The draws below stay inside these ranges and needn't reach their ends.
All inputs are finite; a program needn't handle non-finite values.
Results may differ from the reference program's by a relative error of at most 0.0095.
Values may be sent and summed in bfloat16 or wider, within the bound.
A program may use at most 128 MiB of HBM per device.

```python
import jax
import jax.numpy as jnp
from jax import lax

C = 256
FF = 1024
BLOCKS = 2
NLAT = 60
NLON = 720


def steps_of(rng, shape, shards, low, high):
    gain, own = 1.0, jax.random.fold_in(rng, 6)
    for dim, parts in shards:
        draws = jnp.exp(jax.random.uniform(jax.random.fold_in(own, dim), (parts,), jnp.float32, low / len(shards), high / len(shards)))
        gain = gain * jnp.repeat(draws, shape[dim] // parts).reshape([-1 if axis == dim else 1 for axis in range(len(shape))])
    return gain


def noise(own_key, shape, width, reach, cuts=(), held_as=jnp.bfloat16):
    result = jax.random.normal(own_key, shape, jnp.float32) * width
    if len(cuts) > 0:
        result = steps_of(own_key, shape, cuts, -0.22, 0.18) * result
    return jnp.clip(result, min=-reach, max=reach).astype(held_as)


def setup_inputs(seed: int = 0) -> dict:
    splits = jax.random.split(jax.random.key(seed), 10)
    return {
        "state_field": noise(splits[0], (NLAT, NLON, C), 1.0, 6.0, ((0, 4), (1, 4), (2, 2))),
        "cotangent": noise(splits[1], (NLAT, NLON, C), 1.0, 6.0, ((0, 4), (1, 4), (2, 2))),
        "conv_kernel": noise(splits[2], (BLOCKS, 7, 7, C), 49 ** -0.5, 0.875, ((3, 2),), jnp.float32),
        "conv_bias": noise(splits[3], (BLOCKS, C), 0.5, 3.0, ((1, 2),), jnp.float32),
        "norm_gain": jnp.clip(0.5 + 1.0 * jax.random.uniform(splits[4], (BLOCKS, C), jnp.float32) ** steps_of(splits[4], (BLOCKS, C), ((1, 2),), -0.2, 0.2), 0.5, 1.5),
        "weight_in": noise(splits[5], (BLOCKS, C, FF), C ** -0.5, 0.375),
        "bias_in": noise(splits[6], (BLOCKS, FF), 0.5, 3.0, (), jnp.float32),
        "weight_out": noise(splits[7], (BLOCKS, FF, C), FF ** -0.5, 0.1875),
        "layer_scale": jnp.clip(0.5 + 1.0 * jax.random.uniform(splits[8], (BLOCKS, C), jnp.float32) ** steps_of(splits[8], (BLOCKS, C), ((1, 2),), -0.2, 0.2), 0.5, 1.5),
    }


GELU_SCALE = 0.7978845608028654
CUBIC_TERM = 0.044715
EPSILON = 1e-05

def gelu_value(preact):
    tanh_term = jnp.tanh(GELU_SCALE * (preact + CUBIC_TERM * preact * preact * preact))
    return 0.5 * preact * (1.0 + tanh_term)

def gelu_slope(preact):
    tanh_term = jnp.tanh(GELU_SCALE * (preact + CUBIC_TERM * preact * preact * preact))
    inner = GELU_SCALE * (1.0 + 3.0 * CUBIC_TERM * preact * preact)
    return 0.5 * (1.0 + tanh_term) + 0.5 * preact * (1.0 - tanh_term * tanh_term) * inner

def pad_fold(grid_field):
    half_turn = grid_field.shape[1] // 2
    upper_rows = jnp.roll(grid_field[2::-1], half_turn, axis=1)
    lower_rows = jnp.roll(grid_field[:-4:-1], half_turn, axis=1)
    lat_tall = jnp.concatenate([upper_rows, grid_field, lower_rows], 0)
    return jnp.concatenate([lat_tall[:, -3:], lat_tall, lat_tall[:, :3]], 1)

def depthwise(padded, kernel):
    height = padded.shape[0] - 6
    breadth = padded.shape[1] - 6
    accum = jnp.zeros((height, breadth, padded.shape[2]), jnp.float32)
    for row_tap in range(7):
        for col_tap in range(7):
            accum = accum + padded[row_tap:row_tap + height, col_tap:col_tap + breadth] * kernel[row_tap, col_tap]
    return accum

def normalize(grid_field, kernel, bias_row, gain_row):
    smoothed = depthwise(pad_fold(grid_field.astype(jnp.float32)), kernel) + bias_row
    channels_all = smoothed.shape[-1]
    average = lax.optimization_barrier(jnp.sum(smoothed, -1)) / channels_all
    variance = lax.optimization_barrier(jnp.sum(smoothed * smoothed, -1)) / channels_all - average * average
    inverse_std = lax.rsqrt(variance + EPSILON)
    normed = (smoothed - average[..., None]) * inverse_std[..., None]
    scaled_norm = (normed * gain_row).astype(jnp.bfloat16)
    return (scaled_norm, normed, inverse_std)

def reference(state_field, cotangent, conv_kernel, conv_bias, norm_gain, weight_in, bias_in, weight_out, layer_scale):
    first = normalize(state_field, conv_kernel[0], conv_bias[0], norm_gain[0])

    def mix_row(norm_row):
        preact = jnp.dot(norm_row, weight_in[0], preferred_element_type=jnp.float32) + bias_in[0]
        activated = gelu_value(preact).astype(jnp.bfloat16)
        return jnp.dot(activated, weight_out[0], preferred_element_type=jnp.float32).astype(jnp.bfloat16)
    mixed = lax.map(mix_row, first[0])
    hidden_field = (state_field.astype(jnp.float32) + layer_scale[0] * mixed.astype(jnp.float32)).astype(jnp.bfloat16)
    second = normalize(hidden_field, conv_kernel[1], conv_bias[1], norm_gain[1])
    kept_state = (first, second)
    gradient = cotangent.astype(jnp.float32)
    for block_index in (1, 0):
        scaled_norm, normed, inverse_std = kept_state[block_index]
        grad_mix = (layer_scale[block_index] * gradient).astype(jnp.bfloat16)

        def back_row(row_pair):
            norm_row, grad_row = row_pair
            preact = jnp.dot(norm_row, weight_in[block_index], preferred_element_type=jnp.float32) + bias_in[block_index]
            grad_hidden = jnp.dot(grad_row, weight_out[block_index].T, preferred_element_type=jnp.float32)
            grad_act = (grad_hidden * gelu_slope(preact)).astype(jnp.bfloat16)
            return jnp.dot(grad_act, weight_in[block_index].T, preferred_element_type=jnp.float32).astype(jnp.bfloat16)
        grad_norm = lax.map(back_row, (scaled_norm, grad_mix))
        grad_scaled = grad_norm.astype(jnp.float32) * norm_gain[block_index]
        channels_all = grad_scaled.shape[-1]
        first_mean = lax.optimization_barrier(jnp.sum(grad_scaled, -1)) / channels_all
        second_mean = lax.optimization_barrier(jnp.sum(grad_scaled * normed, -1)) / channels_all
        grad_smooth = (inverse_std[..., None] * (grad_scaled - first_mean[..., None] - normed * second_mean[..., None])).astype(jnp.bfloat16)
        kernel = conv_kernel[block_index]
        unused, adjoint_fn = jax.vjp(lambda probe: depthwise(pad_fold(probe), kernel), jnp.zeros(grad_smooth.shape, jnp.float32))
        gradient = gradient + adjoint_fn(grad_smooth.astype(jnp.float32))[0]
    return gradient
```

```python
import jax
import jax.numpy as jnp
from jax import lax
from jax.sharding import PartitionSpec as P

GELU_SCALE = 0.7978845608028654
CUBIC_TERM = 0.044715
EPSILON = 1e-05


def gelu_value(preact):
    tanh_term = jnp.tanh(GELU_SCALE * (preact + CUBIC_TERM * preact * preact * preact))
    return 0.5 * preact * (1.0 + tanh_term)


def gelu_slope(preact):
    tanh_term = jnp.tanh(GELU_SCALE * (preact + CUBIC_TERM * preact * preact * preact))
    inner = GELU_SCALE * (1.0 + 3.0 * CUBIC_TERM * preact * preact)
    return 0.5 * (1.0 + tanh_term) + 0.5 * preact * (1.0 - tanh_term * tanh_term) * inner


def depthwise(padded, kernel):
    height = padded.shape[0] - 6
    breadth = padded.shape[1] - 6
    accum = jnp.zeros((height, breadth, padded.shape[2]), jnp.float32)
    for row_tap in range(7):
        for col_tap in range(7):
            accum = (
                accum
                + padded[row_tap : row_tap + height, col_tap : col_tap + breadth]
                * kernel[row_tap, col_tap]
            )
    return accum


RING = ("lon", "ch")


def ring_shift(value, steps):
    count = lax.axis_size("lon") * lax.axis_size("ch")
    return lax.ppermute(value, RING, [(i, (i + steps) % count) for i in range(count)])


def lat_shift(value, steps):
    count = lax.axis_size("lat")
    pairs = [(i, i + steps) for i in range(count) if 0 <= i + steps < count]
    return lax.ppermute(value, "lat", pairs)


def swap(value):
    return lax.ppermute(value, "ch", [(0, 1), (1, 0)])


def joined(own, other, first):
    return jnp.where(
        first, jnp.concatenate([own, other], -1), jnp.concatenate([other, own], -1)
    )


def to_cells(field, first):
    half = field.shape[1] // 2
    left, right = field[:, :half], field[:, half:]
    other = swap(jnp.where(first, right, left))
    return joined(jnp.where(first, left, right), other, first)


def to_channels(cells, first):
    half = cells.shape[2] // 2
    low, high = cells[..., :half], cells[..., half:]
    own = jnp.where(first, low, high)
    other = swap(jnp.where(first, high, low))
    return jnp.where(
        first, jnp.concatenate([own, other], 1), jnp.concatenate([other, own], 1)
    )


def padded_field(cells, north_edge, south_edge):
    half_turn = lax.axis_size("lon") * lax.axis_size("ch") // 2
    wide = jnp.concatenate(
        [ring_shift(cells[:, -3:], 1), cells, ring_shift(cells[:, :3], -1)], 1
    )
    folded = ring_shift(jnp.concatenate([wide[2::-1], wide[:-4:-1]], 0), half_turn)
    above = lat_shift(wide[-3:], 1)
    below = lat_shift(wide[:3], -1)
    upper = jnp.where(north_edge, folded[:3], above)
    lower = jnp.where(south_edge, folded[3:], below)
    return lax.optimization_barrier(jnp.concatenate([upper, wide, lower], 0))


def normalize(cells, kernel, bias_row, gain_row, north_edge, south_edge):
    padded = padded_field(cells, north_edge, south_edge).astype(jnp.float32)
    smoothed = depthwise(padded, kernel) + bias_row
    average = jnp.mean(smoothed, -1, keepdims=True)
    variance = jnp.mean(smoothed * smoothed, -1, keepdims=True) - average * average
    inverse_std = lax.rsqrt(variance + EPSILON)
    normed = (smoothed - average) * inverse_std
    return (normed * gain_row).astype(jnp.bfloat16), normed, inverse_std


def adjoint_conv(grad_smooth, kernel, north_edge, south_edge):
    padded = padded_field(grad_smooth, north_edge, south_edge)
    blank = jnp.zeros((3,) + padded.shape[1:], padded.dtype)
    opened = lax.optimization_barrier(
        jnp.concatenate(
            [
                jnp.where(north_edge, blank, padded[:3]),
                padded[3:-3],
                jnp.where(south_edge, blank, padded[-3:]),
            ],
            0,
        )
    )
    result = depthwise(opened.astype(jnp.float32), kernel[::-1, ::-1])
    mirror = kernel[:, ::-1]
    spacer = jnp.zeros((6,) + padded.shape[1:], padded.dtype)
    upper = jnp.concatenate([jnp.where(north_edge, padded[:3], blank), spacer], 0)
    lower = jnp.concatenate([spacer, jnp.where(south_edge, padded[-3:], blank)], 0)
    ends = lax.optimization_barrier((result, upper, lower))
    result, upper, lower = ends
    top = depthwise(upper.astype(jnp.float32), mirror)
    bottom = depthwise(lower.astype(jnp.float32), mirror)
    return jnp.concatenate([result[:3] + top, result[3:-3], result[-3:] + bottom], 0)


def local(
    state_field,
    cotangent,
    conv_kernel,
    conv_bias,
    norm_gain,
    weight_in,
    bias_in,
    weight_out,
    layer_scale,
):
    north_edge = lax.axis_index("lat") == 0
    south_edge = lax.axis_index("lat") == lax.axis_size("lat") - 1
    first = lax.axis_index("ch") == 0
    width = conv_bias.shape[1]
    rows = jnp.concatenate(
        [conv_kernel.reshape(-1, width), conv_bias, norm_gain, layer_scale], 0
    )
    rows = joined(rows, swap(rows), first)
    conv_kernel = rows[:98].reshape(2, 7, 7, 2 * width)
    conv_bias, norm_gain, layer_scale = rows[98:100], rows[100:102], rows[102:104]
    state = to_cells(state_field, first)
    gradient = to_cells(cotangent, first).astype(jnp.float32)
    shape = state.shape

    def matmul(left, right):
        return jnp.dot(left, right, preferred_element_type=jnp.float32)

    kept = []
    inputs = state
    for b in (0, 1):
        scaled, normed, inverse_std = normalize(
            inputs, conv_kernel[b], conv_bias[b], norm_gain[b], north_edge, south_edge
        )
        preact = matmul(scaled.reshape(-1, shape[2]), weight_in[b]) + bias_in[b]
        kept.append((preact, normed, inverse_std))
        if b == 0:
            activated = gelu_value(preact).astype(jnp.bfloat16)
            mixed = matmul(activated, weight_out[0]).astype(jnp.bfloat16).reshape(shape)
            inputs = (
                state.astype(jnp.float32) + layer_scale[0] * mixed.astype(jnp.float32)
            ).astype(jnp.bfloat16)
    for b in (1, 0):
        preact, normed, inverse_std = kept[b]
        grad_mix = (layer_scale[b] * gradient).astype(jnp.bfloat16).reshape(-1, shape[2])
        grad_hidden = matmul(grad_mix, weight_out[b].T)
        grad_act = (grad_hidden * gelu_slope(preact)).astype(jnp.bfloat16)
        grad_norm = matmul(grad_act, weight_in[b].T).astype(jnp.bfloat16).reshape(shape)
        grad_scaled = grad_norm.astype(jnp.float32) * norm_gain[b]
        first_mean = jnp.mean(grad_scaled, -1, keepdims=True)
        second_mean = jnp.mean(grad_scaled * normed, -1, keepdims=True)
        grad_smooth = (
            inverse_std * (grad_scaled - first_mean - normed * second_mean)
        ).astype(jnp.bfloat16)
        gradient = gradient + adjoint_conv(grad_smooth, conv_kernel[b], north_edge, south_edge)
    return to_channels(gradient, first)


def solution(mesh):
    in_specs = (
        P("lat", "lon", "ch"),
        P("lat", "lon", "ch"),
        P(None, None, None, "ch"),
        P(None, "ch"),
        P(None, "ch"),
        P(),
        P(),
        P(),
        P(None, "ch"),
    )
    out_specs = P("lat", "lon", "ch")
    return jax.shard_map(local, mesh=mesh, in_specs=in_specs, out_specs=out_specs, check_vma=False)
```

```python
import functools

import jax
import jax.numpy as jnp
from jax import lax
from jax.experimental import pallas as pl
from jax.experimental.pallas import tpu as pltpu
from jax.sharding import PartitionSpec as P

GELU_SCALE = 0.7978845608028654
CUBIC_TERM = 0.044715
EPSILON = 1e-05
GROUP = 3
SPAN = 32
MESH = pl.DeviceIdType.MESH


def gelu_parts(preact):
    square = preact * preact
    tanh_term = jnp.tanh(GELU_SCALE * preact * (1.0 + CUBIC_TERM * square))
    rise = 0.5 * (1.0 + tanh_term)
    inner = GELU_SCALE * (1.0 + 3.0 * CUBIC_TERM * square)
    slope = rise + 0.5 * preact * (1.0 - tanh_term * tanh_term) * inner
    return preact * rise, slope


def matmul(left, right):
    return jnp.dot(left, right, preferred_element_type=jnp.float32)


def matmul_t(left, right):
    return lax.dot_general(
        left, right, (((1,), (1,)), ((), ())), preferred_element_type=jnp.float32
    )


def body(
    half,
    state_keep,
    state_send,
    cot_keep,
    cot_send,
    param_own,
    weight_in,
    bias_in,
    weight_out,
    out,
    fields,
    cot,
    param,
    edge_out,
    edge_in,
    shifts,
    smoothed,
    normed_kept,
    inverse_kept,
    slope_kept,
    gradient,
    parcel,
    landing,
    send_sem,
    recv_sem,
):
    rows, breadth, lanes = state_keep.shape
    groups = rows // GROUP
    hidden = weight_in.shape[2]
    chunk = hidden // 2
    lon, lat, ch = lax.axis_index("lon"), lax.axis_index("lat"), lax.axis_index("ch")
    lons, lats = lax.axis_size("lon"), lax.axis_size("lat")
    ring = lons * 2
    place = lon * 2 + ch
    north, south = lat == 0, lat == lats - 1
    right, left = lax.rem(place + 1, ring), lax.rem(place + ring - 1, ring)
    opposite = lax.rem(lon + lons // 2, lons)
    partner_id = {"lon": lon, "lat": lat, "ch": 1 - ch}
    right_id = {"lon": right // 2, "lat": lat, "ch": lax.rem(right, 2)}
    left_id = {"lon": left // 2, "lat": lat, "ch": lax.rem(left, 2)}
    up_id = {
        "lon": jnp.where(north, opposite, lon),
        "lat": jnp.where(north, lat, lat - 1),
        "ch": ch,
    }
    down_id = {
        "lon": jnp.where(south, opposite, lon),
        "lat": jnp.where(south, lat, lat + 1),
        "ch": ch,
    }

    def remote(source, target, slot, device, landing_slot=None):
        return pltpu.make_async_remote_copy(
            src_ref=source,
            dst_ref=target,
            send_sem=send_sem.at[slot],
            recv_sem=recv_sem.at[slot if landing_slot is None else landing_slot],
            device_id=device,
            device_id_type=MESH,
        )

    barrier = pltpu.get_barrier_semaphore()
    for device in (right_id, left_id, up_id, down_id):
        pl.semaphore_signal(barrier, inc=1, device_id=device, device_id_type=MESH)
    pl.semaphore_wait(barrier, 4)

    inner = pl.ds(3, rows)
    swaps = [
        remote(param_own, param.at[ch], 0, partner_id),
        remote(state_send, fields.at[0, ch, inner], 1, partner_id),
        remote(cot_send, cot.at[ch], 2, partner_id),
    ]
    for copy in swaps:
        copy.start()
    param[pl.ds(ch, 1)] = param_own[...][None]
    fields[0, pl.ds(ch, 1), inner] = state_keep[...][None]
    cot[pl.ds(ch, 1)] = cot_keep[...][None]
    swaps[0].wait()
    swaps[1].wait()

    spot = lax.broadcasted_iota(jnp.int32, (16, lanes), 0)
    last = breadth - 16
    first_right = half - last

    def turned(value, shift):
        shift = shift % value.shape[0]
        return value if shift == 0 else pltpu.roll(value, shift, 0)

    def send_edges(conv):
        for g in range(2):
            for k in range((rows + 3) // 4):
                packed = [None, None]
                for j in range(4):
                    row = 4 * k + j
                    if row < rows:
                        head = fields[conv, g, 3 + row, 0:16].astype(jnp.float32)
                        tail = fields[conv, g, 3 + row, last:breadth].astype(jnp.float32)
                        pieces = (
                            turned(head, 4 * j),
                            turned(tail, 4 * j - (first_right - 3)),
                        )
                        for way in range(2):
                            if packed[way] is None:
                                packed[way] = pieces[way]
                            else:
                                packed[way] = jnp.where(
                                    spot >= 4 * j, pieces[way], packed[way]
                                )
                for way in range(2):
                    edge_out[conv, way, g, k] = packed[way].astype(jnp.bfloat16)
        copies = [
            remote(edge_out.at[conv, way], edge_in.at[conv, way], 3 + 2 * conv + way, device)
            for way, device in ((0, left_id), (1, right_id))
        ]
        for copy in copies:
            copy.start()
        return copies

    def place_edges(conv):
        for g in range(2):
            for k in range((rows + 3) // 4):
                from_right = edge_in[conv, 0, g, k].astype(jnp.float32)
                from_left = edge_in[conv, 1, g, k].astype(jnp.float32)
                for j in range(4):
                    row = 4 * k + j
                    if row < rows:
                        tile = fields[conv, g, 3 + row, last:breadth].astype(jnp.float32)
                        tile = jnp.where(
                            spot >= first_right, turned(from_right, first_right - 4 * j), tile
                        )
                        tile = jnp.where(spot >= 13, turned(from_left, 13 - 4 * j), tile)
                        fields[conv, g, 3 + row, last:breadth] = tile.astype(jnp.bfloat16)

    def spread(conv, source, row):
        for g in range(2):
            line = fields[conv, g, source].astype(jnp.float32)
            for q in range(7):
                shifts[q, g, row] = turned(line, 3 - q)

    def convolve(conv, block, adjoint, write):
        for copy in send_edges(conv):
            copy.wait()
        place_edges(conv)
        base = 11 + 2 * conv
        upward = remote(
            fields.at[conv, :, pl.ds(3, 3)],
            fields.at[conv, :, pl.ds(jnp.where(north, 0, rows + 3), 3)],
            base,
            up_id,
            jnp.where(north, base, base + 1),
        )
        downward = remote(
            fields.at[conv, :, pl.ds(rows, 3)],
            fields.at[conv, :, pl.ds(jnp.where(south, rows + 3, 0), 3)],
            base + 1,
            down_id,
            jnp.where(south, base + 1, base),
        )
        upward.start()
        downward.start()

        def spread_row(row, carry):
            spread(conv, row + 3, row + 3)
            return carry

        lax.fori_loop(0, rows, spread_row, 0)

        def rows_of(group):
            top = (north & (group == 0)).astype(jnp.int32)
            bottom = (south & (group == groups - 1)).astype(jnp.int32)

            def piece(index, carry):
                g, part = index // (breadth // SPAN), lax.rem(index, breadth // SPAN)
                columns = pl.ds(pl.multiple_of(part * SPAN, SPAN), SPAN)
                sums = [jnp.zeros((SPAN, lanes), jnp.float32) for _ in range(GROUP)]
                for away in range(GROUP + 6):
                    mirror = top if away < 3 else bottom if away >= GROUP + 3 else None
                    for q in range(7):
                        line = shifts[q, g, GROUP * group + away, columns]
                        for i in range(GROUP):
                            p = away - i
                            if 0 <= p <= 6:
                                tap, across = p, q
                                if adjoint:
                                    tap, across = 6 - p, 6 - q
                                    if mirror is not None:
                                        tap = tap + mirror * (2 * p - 6)
                                weight = param[g, block * 7 + tap, across : across + 1]
                                sums[i] = sums[i] + line * weight
                for i in range(GROUP):
                    write(g, GROUP * group + i, columns, sums[i])
                return carry

            lax.fori_loop(0, 2 * (breadth // SPAN), piece, 0)

        def after(group):
            if conv == 3:
                send_rows(group)

        def middle_group(group, carry):
            rows_of(group)
            after(group)
            return carry

        lax.fori_loop(1, groups - 1, middle_group, 0)
        for slot, start in ((base, 0), (base + 1, rows + 3)):
            arrived = fields.at[conv, :, pl.ds(start, 3)]
            remote(arrived, arrived, slot, up_id).wait_recv()
        upward.wait_send()
        downward.wait_send()
        for k in range(3):
            spread(conv, jnp.where(north, 2 - k, k), k)
            spread(conv, jnp.where(south, rows + 5 - k, rows + 3 + k), rows + 3 + k)

        def end_group(index, carry):
            rows_of(index * (groups - 1))
            after(index * (groups - 1))
            return carry

        lax.fori_loop(0, 2, end_group, 0)

    def parcel_copy(group):
        lines = pl.ds(GROUP * group, GROUP)
        return remote(parcel.at[lines], landing.at[lines], 19 + group, partner_id)

    def send_rows(group):
        lines = pl.ds(GROUP * group, GROUP)
        parcel[lines] = gradient[pl.ds(1 - ch, 1), lines][0].astype(jnp.bfloat16)
        parcel_copy(group).start()

    def write_smoothed(g, row, columns, value):
        smoothed[g, row, columns] = value

    def write_gradient_one(g, row, columns, value):
        gradient[g, row, columns] = cot[g, row, columns].astype(jnp.float32) + value

    def write_gradient(g, row, columns, value):
        gradient[g, row, columns] = gradient[g, row, columns] + value

    def wide(ref, lines, *lead):
        parts = [
            ref[(*lead, g, lines)].astype(jnp.float32).reshape(GROUP * breadth, lanes)
            for g in range(2)
        ]
        return jnp.concatenate(parts, -1)

    def row_param(index):
        parts = [param[g, 14, index : index + 1] for g in range(2)]
        return jnp.concatenate(parts, -1)

    def store(conv, group, value):
        for g in range(2):
            part = value[:, g * lanes : (g + 1) * lanes].reshape(GROUP, breadth, lanes)
            fields[conv, g, pl.ds(3 + GROUP * group, GROUP)] = part

    def norm_of(group, block):
        value = wide(smoothed, pl.ds(GROUP * group, GROUP)) + row_param(block)
        average = jnp.mean(value, -1, keepdims=True)
        variance = jnp.mean(value * value, -1, keepdims=True) - average * average
        inverse_std = lax.rsqrt(variance + EPSILON)
        normed = (value - average) * inverse_std
        return normed, inverse_std, (normed * row_param(2 + block)).astype(jnp.bfloat16)

    def backward(grad_norm, normed, inverse_std, block):
        grad_scaled = grad_norm.astype(jnp.bfloat16).astype(jnp.float32) * row_param(2 + block)
        first_mean = jnp.mean(grad_scaled, -1, keepdims=True)
        second_mean = jnp.mean(grad_scaled * normed, -1, keepdims=True)
        return (inverse_std * (grad_scaled - first_mean - normed * second_mean)).astype(
            jnp.bfloat16
        )

    def spans():
        return [slice(k * chunk, (k + 1) * chunk) for k in range(2)]

    def first_forward(group, carry):
        normed, inverse_std, scaled = norm_of(group, 0)
        normed_kept[group] = normed
        inverse_kept[group] = inverse_std
        total = None
        for span in spans():
            preact = matmul(scaled, weight_in[0, :, span]) + bias_in[0:1, span]
            value, slope = gelu_parts(preact)
            slope_kept[group, :, span] = slope
            term = matmul(value.astype(jnp.bfloat16), weight_out[0, span])
            total = term if total is None else total + term
        mixed = total.astype(jnp.bfloat16).astype(jnp.float32)
        state = wide(fields, pl.ds(3 + GROUP * group, GROUP), 0)
        store(1, group, (state + row_param(4) * mixed).astype(jnp.bfloat16))
        return carry

    def second_both(group, carry):
        normed, inverse_std, scaled = norm_of(group, 1)
        grad_mix = (wide(cot, pl.ds(GROUP * group, GROUP)) * row_param(5)).astype(jnp.bfloat16)
        total = None
        for span in spans():
            preact = matmul(scaled, weight_in[1, :, span]) + bias_in[1:2, span]
            slope = gelu_parts(preact)[1]
            grad_act = (matmul_t(grad_mix, weight_out[1, span]) * slope).astype(jnp.bfloat16)
            term = matmul_t(grad_act, weight_in[1, :, span])
            total = term if total is None else total + term
        store(2, group, backward(total, normed, inverse_std, 1))
        return carry

    def first_backward(group, carry):
        grad_mix = (wide(gradient, pl.ds(GROUP * group, GROUP)) * row_param(4)).astype(
            jnp.bfloat16
        )
        total = None
        for span in spans():
            grad_hidden = matmul_t(grad_mix, weight_out[0, span])
            grad_act = (grad_hidden * slope_kept[group, :, span]).astype(jnp.bfloat16)
            term = matmul_t(grad_act, weight_in[0, :, span])
            total = term if total is None else total + term
        store(3, group, backward(total, normed_kept[group], inverse_kept[group], 0))
        return carry

    convolve(0, 0, False, write_smoothed)
    lax.fori_loop(0, groups, first_forward, 0)
    convolve(1, 1, False, write_smoothed)
    swaps[2].wait()
    lax.fori_loop(0, groups, second_both, 0)
    convolve(2, 1, True, write_gradient_one)
    lax.fori_loop(0, groups, first_backward, 0)
    convolve(3, 0, True, write_gradient)
    out[pl.ds(ch, 1)] = gradient[pl.ds(ch, 1)]
    for group in range(groups):
        parcel_copy(group).wait()
    out[pl.ds(1 - ch, 1)] = landing[...].astype(jnp.float32)[None]


def local(
    state_field,
    cotangent,
    conv_kernel,
    conv_bias,
    norm_gain,
    weight_in,
    bias_in,
    weight_out,
    layer_scale,
):
    first = lax.axis_index("ch") == 0
    rows, columns, lanes = state_field.shape
    half = columns // 2
    breadth = half + 6
    assert breadth % SPAN == 0 and rows % GROUP == 0 and lax.axis_size("ch") == 2

    def halves(field):
        parts = field[:, :half], field[:, half:]
        grow = ((0, 0), (0, breadth - half), (0, 0))
        return (
            jnp.pad(jnp.where(first, *parts), grow),
            jnp.pad(jnp.where(first, *parts[::-1]), grow),
        )

    taps = jnp.pad(conv_kernel, ((0, 0), (0, 0), (0, 1), (0, 0))).reshape(14, 8, lanes)
    rest = jnp.concatenate([conv_bias, norm_gain, layer_scale, layer_scale], 0)[None]
    param = jnp.concatenate([taps, rest], 0)
    groups = rows // GROUP
    hidden = weight_in.shape[2]
    cells = GROUP * breadth
    vmem = pl.BlockSpec(memory_space=pltpu.VMEM)
    result = pl.pallas_call(
        functools.partial(body, half),
        out_shape=jax.ShapeDtypeStruct((2, rows, breadth, lanes), jnp.float32),
        in_specs=[vmem] * 8,
        out_specs=vmem,
        scratch_shapes=[
            pltpu.VMEM((4, 2, rows + 6, breadth, lanes), jnp.bfloat16),
            pltpu.VMEM((2, rows, breadth, lanes), jnp.bfloat16),
            pltpu.VMEM((2, 15, 8, lanes), jnp.float32),
            pltpu.VMEM((4, 2, 2, (rows + 3) // 4, 16, lanes), jnp.bfloat16),
            pltpu.VMEM((4, 2, 2, (rows + 3) // 4, 16, lanes), jnp.bfloat16),
            pltpu.VMEM((7, 2, rows + 6, breadth, lanes), jnp.float32),
            pltpu.VMEM((2, rows, breadth, lanes), jnp.float32),
            pltpu.VMEM((groups, cells, 2 * lanes), jnp.float32),
            pltpu.VMEM((groups, cells, 1), jnp.float32),
            pltpu.VMEM((groups, cells, hidden), jnp.float32),
            pltpu.VMEM((2, rows, breadth, lanes), jnp.float32),
            pltpu.VMEM((rows, breadth, lanes), jnp.bfloat16),
            pltpu.VMEM((rows, breadth, lanes), jnp.bfloat16),
            pltpu.SemaphoreType.DMA((19 + groups,)),
            pltpu.SemaphoreType.DMA((19 + groups,)),
        ],
        compiler_params=pltpu.CompilerParams(
            collective_id=0, has_side_effects=True, vmem_limit_bytes=60 * 1024 * 1024
        ),
    )(*halves(state_field), *halves(cotangent), param, weight_in, bias_in, weight_out)
    return jnp.concatenate([result[0, :, :half], result[1, :, :half]], 1)


def solution(mesh):
    in_specs = (
        P("lat", "lon", "ch"),
        P("lat", "lon", "ch"),
        P(None, None, None, "ch"),
        P(None, "ch"),
        P(None, "ch"),
        P(),
        P(),
        P(),
        P(None, "ch"),
    )
    out_specs = P("lat", "lon", "ch")
    return jax.shard_map(local, mesh=mesh, in_specs=in_specs, out_specs=out_specs, check_vma=False)
```

```python
import functools

import jax
import jax.numpy as jnp
from jax import lax
from jax.experimental import pallas as pl
from jax.experimental.pallas import tpu as pltpu
from jax.sharding import PartitionSpec as P

GELU_SCALE = 0.7978845608028654
CUBIC_TERM = 0.044715
EPSILON = 1e-05
GROUP = 3
SPAN = 32
MESH = pl.DeviceIdType.MESH


def gelu_parts(preact):
    square = preact * preact
    tanh_term = jnp.tanh(GELU_SCALE * preact * (1.0 + CUBIC_TERM * square))
    rise = 0.5 * (1.0 + tanh_term)
    inner = GELU_SCALE * (1.0 + 3.0 * CUBIC_TERM * square)
    slope = rise + 0.5 * preact * (1.0 - tanh_term * tanh_term) * inner
    return preact * rise, slope


def matmul(left, right):
    return jnp.dot(left, right, preferred_element_type=jnp.float32)


def matmul_t(left, right):
    return lax.dot_general(
        left, right, (((1,), (1,)), ((), ())), preferred_element_type=jnp.float32
    )


def body(
    half,
    state_keep,
    state_send,
    cot_keep,
    cot_send,
    param_own,
    weight_in,
    bias_in,
    weight_out,
    out,
    fields,
    cot,
    param,
    edge_out,
    edge_in,
    shifts,
    smoothed,
    normed_kept,
    inverse_kept,
    slope_kept,
    gradient,
    parcel,
    landing,
    send_sem,
    recv_sem,
):
    rows, breadth, lanes = state_keep.shape
    groups = rows // GROUP
    row_base = 2
    state_base = row_base + 8
    parcel_base = state_base + groups
    edge_base = parcel_base + groups
    hidden = weight_in.shape[2]
    chunk = hidden // 2
    lon, lat, ch = lax.axis_index("lon"), lax.axis_index("lat"), lax.axis_index("ch")
    lons, lats = lax.axis_size("lon"), lax.axis_size("lat")
    ring = lons * 2
    place = lon * 2 + ch
    north, south = lat == 0, lat == lats - 1
    right, left = lax.rem(place + 1, ring), lax.rem(place + ring - 1, ring)
    opposite = lax.rem(lon + lons // 2, lons)
    partner_id = {"lon": lon, "lat": lat, "ch": 1 - ch}
    right_id = {"lon": right // 2, "lat": lat, "ch": lax.rem(right, 2)}
    left_id = {"lon": left // 2, "lat": lat, "ch": lax.rem(left, 2)}
    up_id = {
        "lon": jnp.where(north, opposite, lon),
        "lat": jnp.where(north, lat, lat - 1),
        "ch": ch,
    }
    down_id = {
        "lon": jnp.where(south, opposite, lon),
        "lat": jnp.where(south, lat, lat + 1),
        "ch": ch,
    }

    def remote(source, target, slot, device, landing_slot=None):
        return pltpu.make_async_remote_copy(
            src_ref=source,
            dst_ref=target,
            send_sem=send_sem.at[slot],
            recv_sem=recv_sem.at[slot if landing_slot is None else landing_slot],
            device_id=device,
            device_id_type=MESH,
        )

    barrier = pltpu.get_barrier_semaphore()
    for device in (right_id, left_id, up_id, down_id):
        pl.semaphore_signal(barrier, inc=1, device_id=device, device_id_type=MESH)
    pl.semaphore_wait(barrier, 4)

    inner = pl.ds(3, rows)
    swaps = [
        remote(param_own, param.at[ch], 0, partner_id),
        remote(cot_send, cot.at[ch], 1, partner_id),
    ]

    def state_swap(group):
        lines = pl.ds(GROUP * group, GROUP)
        return remote(
            state_send.at[lines],
            fields.at[0, ch, pl.ds(3 + GROUP * group, GROUP)],
            state_base + group,
            partner_id,
        )

    def order(step):
        return jnp.where(step == 0, 0, jnp.where(step == 1, groups - 1, step - 1))

    for step in range(groups):
        state_swap(0 if step == 0 else groups - 1 if step == 1 else step - 1).start()
    swaps[0].start()
    param[pl.ds(ch, 1)] = param_own[...][None]
    fields[0, pl.ds(ch, 1), inner] = state_keep[...][None]
    cot[pl.ds(ch, 1)] = cot_keep[...][None]

    spot = lax.broadcasted_iota(jnp.int32, (16, lanes), 0)
    last = breadth - 16
    first_right = half - last

    def turned(value, shift):
        shift = shift % value.shape[0]
        return value if shift == 0 else pltpu.roll(value, shift, 0)

    def edge_copies(conv, group):
        return [
            remote(
                edge_out.at[conv, way, group],
                edge_in.at[conv, way, group],
                edge_base + (2 * conv + way) * groups + group,
                device,
            )
            for way, device in ((0, left_id), (1, right_id))
        ]

    def send_edges(conv, group):
        for g in range(2):
            packed = [None, None]
            for j in range(GROUP):
                row = 3 + GROUP * group + j
                head = fields[conv, g, row, 0:16].astype(jnp.float32)
                tail = fields[conv, g, row, last:breadth].astype(jnp.float32)
                pieces = (
                    turned(head, 4 * j),
                    turned(tail, 4 * j - (first_right - 3)),
                )
                for way in range(2):
                    if packed[way] is None:
                        packed[way] = pieces[way]
                    else:
                        packed[way] = jnp.where(spot >= 4 * j, pieces[way], packed[way])
            for way in range(2):
                edge_out[conv, way, group, g] = packed[way].astype(jnp.bfloat16)
        for copy in edge_copies(conv, group):
            copy.start()

    def place_edges(conv, group):
        for copy in edge_copies(conv, group):
            copy.wait()
        for g in range(2):
            from_right = edge_in[conv, 0, group, g].astype(jnp.float32)
            from_left = edge_in[conv, 1, group, g].astype(jnp.float32)
            for j in range(GROUP):
                row = 3 + GROUP * group + j
                tile = fields[conv, g, row, last:breadth].astype(jnp.float32)
                tile = jnp.where(
                    spot >= first_right, turned(from_right, first_right - 4 * j), tile
                )
                tile = jnp.where(spot >= 13, turned(from_left, 13 - 4 * j), tile)
                fields[conv, g, row, last:breadth] = tile.astype(jnp.bfloat16)

    def row_copies(conv):
        base = row_base + 2 * conv
        return (
            remote(
                fields.at[conv, :, pl.ds(3, 3)],
                fields.at[conv, :, pl.ds(jnp.where(north, 0, rows + 3), 3)],
                base,
                up_id,
                jnp.where(north, base, base + 1),
            ),
            remote(
                fields.at[conv, :, pl.ds(rows, 3)],
                fields.at[conv, :, pl.ds(jnp.where(south, rows + 3, 0), 3)],
                base + 1,
                down_id,
                jnp.where(south, base + 1, base),
            ),
        )

    def produce(conv, make):
        def step_of(step, carry):
            group = order(step)
            make(group)
            send_edges(conv, group)

            @pl.when(step == 2)
            def _():
                place_edges(conv, 0)
                place_edges(conv, groups - 1)
                for copy in row_copies(conv):
                    copy.start()

            return carry

        lax.fori_loop(0, groups, step_of, 0)

    def spread(conv, source, row):
        for g in range(2):
            line = fields[conv, g, source].astype(jnp.float32)
            for q in range(7):
                shifts[q, g, row] = turned(line, 3 - q)

    def convolve(conv, block, adjoint, write):
        def take_group(group, carry):
            @pl.when((group > 0) & (group < groups - 1))
            def _():
                place_edges(conv, group)

            def spread_row(row, inner_carry):
                spread(conv, row, row)
                return inner_carry

            return lax.fori_loop(3 + GROUP * group, 3 + GROUP * (group + 1), spread_row, carry)

        lax.fori_loop(0, groups, take_group, 0)

        def rows_of(group, only=None):
            top = (north & (group == 0)).astype(jnp.int32)
            bottom = (south & (group == groups - 1)).astype(jnp.int32)

            def piece(index, carry):
                g, part = index // (breadth // SPAN), lax.rem(index, breadth // SPAN)
                if only is not None:
                    g = only
                columns = pl.ds(pl.multiple_of(part * SPAN, SPAN), SPAN)
                sums = [jnp.zeros((SPAN, lanes), jnp.float32) for _ in range(GROUP)]
                for away in range(GROUP + 6):
                    mirror = top if away < 3 else bottom if away >= GROUP + 3 else None
                    for q in range(7):
                        line = shifts[q, g, GROUP * group + away, columns]
                        for i in range(GROUP):
                            p = away - i
                            if 0 <= p <= 6:
                                tap, across = p, q
                                if adjoint:
                                    tap, across = 6 - p, 6 - q
                                    if mirror is not None:
                                        tap = tap + mirror * (2 * p - 6)
                                weight = param[g, block * 7 + tap, across : across + 1]
                                sums[i] = sums[i] + line * weight
                for i in range(GROUP):
                    write(g, GROUP * group + i, columns, sums[i])
                return carry

            count = 2 if only is None else 1
            lax.fori_loop(0, count * (breadth // SPAN), piece, 0)

        firsts = 1 - ch if adjoint and block == 0 else None

        def work(group, only, send):
            rows_of(group, only)
            if send:
                send_rows(group)

        def middle(only, send):
            def step(group, carry):
                work(group, only, send)
                return carry

            lax.fori_loop(1, groups - 1, step, 0)

        def ends(only, send):
            def step(index, carry):
                work(index * (groups - 1), only, send)
                return carry

            lax.fori_loop(0, 2, step, 0)

        middle(firsts, firsts is not None)
        base = row_base + 2 * conv
        for slot, start in ((base, 0), (base + 1, rows + 3)):
            arrived = fields.at[conv, :, pl.ds(start, 3)]
            remote(arrived, arrived, slot, up_id).wait_recv()
        for copy in row_copies(conv):
            copy.wait_send()
        if conv == 0:
            swaps[1].start()
        for k in range(3):
            spread(conv, jnp.where(north, 2 - k, k), k)
            spread(conv, jnp.where(south, rows + 5 - k, rows + 3 + k), rows + 3 + k)
        ends(firsts, firsts is not None)
        if firsts is not None:
            def own_step(group, carry):
                rows_of(group, ch)
                return carry

            lax.fori_loop(0, groups, own_step, 0)

    def parcel_copy(group):
        lines = pl.ds(GROUP * group, GROUP)
        return remote(parcel.at[lines], landing.at[lines], parcel_base + group, partner_id)

    def send_rows(group):
        lines = pl.ds(GROUP * group, GROUP)
        parcel[lines] = gradient[pl.ds(1 - ch, 1), lines][0].astype(jnp.bfloat16)
        parcel_copy(group).start()

    def write_smoothed(g, row, columns, value):
        smoothed[g, row, columns] = value

    def write_gradient_one(g, row, columns, value):
        gradient[g, row, columns] = cot[g, row, columns].astype(jnp.float32) + value

    def write_gradient(g, row, columns, value):
        gradient[g, row, columns] = gradient[g, row, columns] + value

    def wide(ref, lines, *lead):
        parts = [
            ref[(*lead, g, lines)].astype(jnp.float32).reshape(GROUP * breadth, lanes)
            for g in range(2)
        ]
        return jnp.concatenate(parts, -1)

    def row_param(index):
        parts = [param[g, 14, index : index + 1] for g in range(2)]
        return jnp.concatenate(parts, -1)

    def store(conv, group, value):
        for g in range(2):
            part = value[:, g * lanes : (g + 1) * lanes].reshape(GROUP, breadth, lanes)
            fields[conv, g, pl.ds(3 + GROUP * group, GROUP)] = part

    def norm_of(group, block):
        value = wide(smoothed, pl.ds(GROUP * group, GROUP)) + row_param(block)
        average = jnp.mean(value, -1, keepdims=True)
        variance = jnp.mean(value * value, -1, keepdims=True) - average * average
        inverse_std = lax.rsqrt(variance + EPSILON)
        normed = (value - average) * inverse_std
        return normed, inverse_std, (normed * row_param(2 + block)).astype(jnp.bfloat16)

    def backward(grad_norm, normed, inverse_std, block):
        grad_scaled = grad_norm.astype(jnp.bfloat16).astype(jnp.float32) * row_param(2 + block)
        first_mean = jnp.mean(grad_scaled, -1, keepdims=True)
        second_mean = jnp.mean(grad_scaled * normed, -1, keepdims=True)
        return (inverse_std * (grad_scaled - first_mean - normed * second_mean)).astype(
            jnp.bfloat16
        )

    def spans():
        return [slice(k * chunk, (k + 1) * chunk) for k in range(2)]

    def first_forward(group):
        normed, inverse_std, scaled = norm_of(group, 0)
        normed_kept[group] = normed
        inverse_kept[group] = inverse_std
        total = None
        for span in spans():
            preact = matmul(scaled, weight_in[0, :, span]) + bias_in[0:1, span]
            value, slope = gelu_parts(preact)
            slope_kept[group, :, span] = slope
            term = matmul(value.astype(jnp.bfloat16), weight_out[0, span])
            total = term if total is None else total + term
        mixed = total.astype(jnp.bfloat16).astype(jnp.float32)
        state = wide(fields, pl.ds(3 + GROUP * group, GROUP), 0)
        store(1, group, (state + row_param(4) * mixed).astype(jnp.bfloat16))

    def second_both(group):
        normed, inverse_std, scaled = norm_of(group, 1)
        grad_mix = (wide(cot, pl.ds(GROUP * group, GROUP)) * row_param(5)).astype(jnp.bfloat16)
        total = None
        for span in spans():
            preact = matmul(scaled, weight_in[1, :, span]) + bias_in[1:2, span]
            slope = gelu_parts(preact)[1]
            grad_act = (matmul_t(grad_mix, weight_out[1, span]) * slope).astype(jnp.bfloat16)
            term = matmul_t(grad_act, weight_in[1, :, span])
            total = term if total is None else total + term
        store(2, group, backward(total, normed, inverse_std, 1))

    def first_backward(group):
        grad_mix = (wide(gradient, pl.ds(GROUP * group, GROUP)) * row_param(4)).astype(
            jnp.bfloat16
        )
        total = None
        for span in spans():
            grad_hidden = matmul_t(grad_mix, weight_out[0, span])
            grad_act = (grad_hidden * slope_kept[group, :, span]).astype(jnp.bfloat16)
            term = matmul_t(grad_act, weight_in[0, :, span])
            total = term if total is None else total + term
        store(3, group, backward(total, normed_kept[group], inverse_kept[group], 0))

    produce(0, lambda group: state_swap(group).wait())
    swaps[0].wait()
    convolve(0, 0, False, write_smoothed)
    produce(1, first_forward)
    convolve(1, 1, False, write_smoothed)
    swaps[1].wait()
    produce(2, second_both)
    convolve(2, 1, True, write_gradient_one)
    produce(3, first_backward)
    convolve(3, 0, True, write_gradient)
    out[pl.ds(ch, 1)] = gradient[pl.ds(ch, 1)]
    for group in range(groups):
        parcel_copy(group).wait()
    out[pl.ds(1 - ch, 1)] = landing[...].astype(jnp.float32)[None]


def local(
    state_field,
    cotangent,
    conv_kernel,
    conv_bias,
    norm_gain,
    weight_in,
    bias_in,
    weight_out,
    layer_scale,
):
    first = lax.axis_index("ch") == 0
    rows, columns, lanes = state_field.shape
    half = columns // 2
    breadth = half + 6
    assert breadth % SPAN == 0 and rows % GROUP == 0 and lax.axis_size("ch") == 2

    def halves(field):
        parts = field[:, :half], field[:, half:]
        grow = ((0, 0), (0, breadth - half), (0, 0))
        return (
            jnp.pad(jnp.where(first, *parts), grow),
            jnp.pad(jnp.where(first, *parts[::-1]), grow),
        )

    taps = jnp.pad(conv_kernel, ((0, 0), (0, 0), (0, 1), (0, 0))).reshape(14, 8, lanes)
    rest = jnp.concatenate([conv_bias, norm_gain, layer_scale, layer_scale], 0)[None]
    param = jnp.concatenate([taps, rest], 0)
    groups = rows // GROUP
    hidden = weight_in.shape[2]
    cells = GROUP * breadth
    vmem = pl.BlockSpec(memory_space=pltpu.VMEM)
    result = pl.pallas_call(
        functools.partial(body, half),
        out_shape=jax.ShapeDtypeStruct((2, rows, breadth, lanes), jnp.float32),
        in_specs=[vmem] * 8,
        out_specs=vmem,
        scratch_shapes=[
            pltpu.VMEM((4, 2, rows + 6, breadth, lanes), jnp.bfloat16),
            pltpu.VMEM((2, rows, breadth, lanes), jnp.bfloat16),
            pltpu.VMEM((2, 15, 8, lanes), jnp.float32),
            pltpu.VMEM((4, 2, groups, 2, 16, lanes), jnp.bfloat16),
            pltpu.VMEM((4, 2, groups, 2, 16, lanes), jnp.bfloat16),
            pltpu.VMEM((7, 2, rows + 6, breadth, lanes), jnp.float32),
            pltpu.VMEM((2, rows, breadth, lanes), jnp.float32),
            pltpu.VMEM((groups, cells, 2 * lanes), jnp.float32),
            pltpu.VMEM((groups, cells, 1), jnp.float32),
            pltpu.VMEM((groups, cells, hidden), jnp.float32),
            pltpu.VMEM((2, rows, breadth, lanes), jnp.float32),
            pltpu.VMEM((rows, breadth, lanes), jnp.bfloat16),
            pltpu.VMEM((rows, breadth, lanes), jnp.bfloat16),
            pltpu.SemaphoreType.DMA((10 + 10 * groups,)),
            pltpu.SemaphoreType.DMA((10 + 10 * groups,)),
        ],
        compiler_params=pltpu.CompilerParams(
            collective_id=0, has_side_effects=True, vmem_limit_bytes=60 * 1024 * 1024
        ),
    )(*halves(state_field), *halves(cotangent), param, weight_in, bias_in, weight_out)
    return jnp.concatenate([result[0, :, :half], result[1, :, :half]], 1)


def solution(mesh):
    in_specs = (
        P("lat", "lon", "ch"),
        P("lat", "lon", "ch"),
        P(None, None, None, "ch"),
        P(None, "ch"),
        P(None, "ch"),
        P(),
        P(),
        P(),
        P(None, "ch"),
    )
    out_specs = P("lat", "lon", "ch")
    return jax.shard_map(local, mesh=mesh, in_specs=in_specs, out_specs=out_specs, check_vma=False)
```

```python
import functools

import jax
import jax.numpy as jnp
from jax import lax
from jax.experimental import pallas as pl
from jax.experimental.pallas import tpu as pltpu
from jax.sharding import PartitionSpec as P

GELU_SCALE = 0.7978845608028654
CUBIC_TERM = 0.044715
EPSILON = 1e-05
GROUP = 3
SPAN = 32
MESH = pl.DeviceIdType.MESH


def gelu_parts(preact):
    square = preact * preact
    tanh_term = jnp.tanh(GELU_SCALE * preact * (1.0 + CUBIC_TERM * square))
    rise = 0.5 * (1.0 + tanh_term)
    inner = GELU_SCALE * (1.0 + 3.0 * CUBIC_TERM * square)
    slope = rise + 0.5 * preact * (1.0 - tanh_term * tanh_term) * inner
    return preact * rise, slope


def matmul(left, right):
    return jnp.dot(left, right, preferred_element_type=jnp.float32)


def matmul_t(left, right):
    return lax.dot_general(
        left, right, (((1,), (1,)), ((), ())), preferred_element_type=jnp.float32
    )


def body(
    half,
    state_keep,
    state_send,
    cot_keep,
    cot_send,
    param_own,
    weight_in,
    bias_in,
    weight_out,
    out,
    fields,
    cot,
    param,
    edge_out,
    edge_in,
    shifts,
    smoothed,
    normed_kept,
    inverse_kept,
    slope_kept,
    gradient,
    parcel,
    landing,
    send_sem,
    recv_sem,
):
    rows, breadth, lanes = state_keep.shape
    groups = rows // GROUP
    row_base = 2
    state_base = row_base + 8
    parcel_base = state_base + groups
    edge_base = parcel_base + groups
    hidden = weight_in.shape[2]
    chunk = hidden // 2
    lon, lat, ch = lax.axis_index("lon"), lax.axis_index("lat"), lax.axis_index("ch")
    lons, lats = lax.axis_size("lon"), lax.axis_size("lat")
    ring = lons * 2
    place = lon * 2 + ch
    north, south = lat == 0, lat == lats - 1
    right, left = lax.rem(place + 1, ring), lax.rem(place + ring - 1, ring)
    opposite = lax.rem(lon + lons // 2, lons)
    partner_id = {"lon": lon, "lat": lat, "ch": 1 - ch}
    right_id = {"lon": right // 2, "lat": lat, "ch": lax.rem(right, 2)}
    left_id = {"lon": left // 2, "lat": lat, "ch": lax.rem(left, 2)}
    up_id = {
        "lon": jnp.where(north, opposite, lon),
        "lat": jnp.where(north, lat, lat - 1),
        "ch": ch,
    }
    down_id = {
        "lon": jnp.where(south, opposite, lon),
        "lat": jnp.where(south, lat, lat + 1),
        "ch": ch,
    }

    def remote(source, target, slot, device, landing_slot=None):
        return pltpu.make_async_remote_copy(
            src_ref=source,
            dst_ref=target,
            send_sem=send_sem.at[slot],
            recv_sem=recv_sem.at[slot if landing_slot is None else landing_slot],
            device_id=device,
            device_id_type=MESH,
        )

    barrier = pltpu.get_barrier_semaphore()
    for device in (right_id, left_id, up_id, down_id):
        pl.semaphore_signal(barrier, inc=1, device_id=device, device_id_type=MESH)
    pl.semaphore_wait(barrier, 4)

    inner = pl.ds(3, rows)
    swaps = [
        remote(param_own, param.at[ch], 0, partner_id),
        remote(cot_send, cot.at[ch], 1, partner_id),
    ]

    def state_swap(group):
        lines = pl.ds(GROUP * group, GROUP)
        return remote(
            state_send.at[lines],
            fields.at[0, ch, pl.ds(3 + GROUP * group, GROUP)],
            state_base + group,
            partner_id,
        )

    def order(step):
        return jnp.where(step == 0, 0, jnp.where(step == 1, groups - 1, step - 1))

    for step in range(groups):
        state_swap(0 if step == 0 else groups - 1 if step == 1 else step - 1).start()
    swaps[0].start()
    param[pl.ds(ch, 1)] = param_own[...][None]
    fields[0, pl.ds(ch, 1), inner] = state_keep[...][None]
    cot[pl.ds(ch, 1)] = cot_keep[...][None]

    spot = lax.broadcasted_iota(jnp.int32, (16, lanes), 0)
    last = breadth - 16
    first_right = half - last

    def turned(value, shift):
        shift = shift % value.shape[0]
        return value if shift == 0 else pltpu.roll(value, shift, 0)

    def edge_copies(conv, group):
        return [
            remote(
                edge_out.at[conv, way, group],
                edge_in.at[conv, way, group],
                edge_base + (2 * conv + way) * groups + group,
                device,
            )
            for way, device in ((0, left_id), (1, right_id))
        ]

    def send_edges(conv, group):
        for g in range(2):
            packed = [None, None]
            for j in range(GROUP):
                row = 3 + GROUP * group + j
                head = fields[conv, g, row, 0:16].astype(jnp.float32)
                tail = fields[conv, g, row, last:breadth].astype(jnp.float32)
                pieces = (
                    turned(head, 4 * j),
                    turned(tail, 4 * j - (first_right - 3)),
                )
                for way in range(2):
                    if packed[way] is None:
                        packed[way] = pieces[way]
                    else:
                        packed[way] = jnp.where(spot >= 4 * j, pieces[way], packed[way])
            for way in range(2):
                edge_out[conv, way, group, g] = packed[way].astype(jnp.bfloat16)
        for copy in edge_copies(conv, group):
            copy.start()

    def place_edges(conv, group):
        for copy in edge_copies(conv, group):
            copy.wait()
        for g in range(2):
            from_right = edge_in[conv, 0, group, g].astype(jnp.float32)
            from_left = edge_in[conv, 1, group, g].astype(jnp.float32)
            for j in range(GROUP):
                row = 3 + GROUP * group + j
                tile = fields[conv, g, row, last:breadth].astype(jnp.float32)
                tile = jnp.where(
                    spot >= first_right, turned(from_right, first_right - 4 * j), tile
                )
                tile = jnp.where(spot >= 13, turned(from_left, 13 - 4 * j), tile)
                fields[conv, g, row, last:breadth] = tile.astype(jnp.bfloat16)

    def row_copies(conv):
        base = row_base + 2 * conv
        return (
            remote(
                fields.at[conv, :, pl.ds(3, 3)],
                fields.at[conv, :, pl.ds(jnp.where(north, 0, rows + 3), 3)],
                base,
                up_id,
                jnp.where(north, base, base + 1),
            ),
            remote(
                fields.at[conv, :, pl.ds(rows, 3)],
                fields.at[conv, :, pl.ds(jnp.where(south, rows + 3, 0), 3)],
                base + 1,
                down_id,
                jnp.where(south, base + 1, base),
            ),
        )

    def produce(conv, make):
        def step_of(step, carry):
            group = order(step)
            make(group)
            send_edges(conv, group)

            @pl.when(step == 2)
            def _():
                place_edges(conv, 0)
                place_edges(conv, groups - 1)
                for copy in row_copies(conv):
                    copy.start()

            return carry

        lax.fori_loop(0, groups, step_of, 0)

    def spread(conv, source, row):
        for g in range(2):
            line = fields[conv, g, source].astype(jnp.float32)
            for q in range(7):
                shifts[q, g, row] = turned(line, 3 - q)

    def convolve(conv, block, adjoint, write):
        def take_group(group, carry):
            @pl.when((group > 0) & (group < groups - 1))
            def _():
                place_edges(conv, group)

            def spread_row(row, inner_carry):
                spread(conv, row, row)
                return inner_carry

            return lax.fori_loop(3 + GROUP * group, 3 + GROUP * (group + 1), spread_row, carry)

        lax.fori_loop(0, groups, take_group, 0)

        def rows_of(group, only=None):
            top = (north & (group == 0)).astype(jnp.int32)
            bottom = (south & (group == groups - 1)).astype(jnp.int32)

            def piece(index, carry):
                g, part = index // (breadth // SPAN), lax.rem(index, breadth // SPAN)
                if only is not None:
                    g = only
                columns = pl.ds(pl.multiple_of(part * SPAN, SPAN), SPAN)
                sums = [jnp.zeros((SPAN, lanes), jnp.float32) for _ in range(GROUP)]
                for away in range(GROUP + 6):
                    mirror = top if away < 3 else bottom if away >= GROUP + 3 else None
                    for q in range(7):
                        line = shifts[q, g, GROUP * group + away, columns]
                        for i in range(GROUP):
                            p = away - i
                            if 0 <= p <= 6:
                                tap, across = p, q
                                if adjoint:
                                    tap, across = 6 - p, 6 - q
                                    if mirror is not None:
                                        tap = tap + mirror * (2 * p - 6)
                                weight = param[g, block * 7 + tap, across : across + 1]
                                sums[i] = sums[i] + line * weight
                for i in range(GROUP):
                    write(g, GROUP * group + i, columns, sums[i])
                return carry

            count = 2 if only is None else 1
            lax.fori_loop(0, count * (breadth // SPAN), piece, 0)

        firsts = 1 - ch if adjoint and block == 0 else None

        def work(group, only, send):
            rows_of(group, only)
            if send:
                send_rows(group)

        def middle(only, send):
            def step(group, carry):
                work(group, only, send)
                return carry

            lax.fori_loop(1, groups - 1, step, 0)

        def ends(only, send):
            def step(index, carry):
                work(index * (groups - 1), only, send)
                return carry

            lax.fori_loop(0, 2, step, 0)

        middle(firsts, firsts is not None)
        base = row_base + 2 * conv
        for slot, start in ((base, 0), (base + 1, rows + 3)):
            arrived = fields.at[conv, :, pl.ds(start, 3)]
            remote(arrived, arrived, slot, up_id).wait_recv()
        for copy in row_copies(conv):
            copy.wait_send()
        if conv == 0:
            swaps[1].start()
        for k in range(3):
            spread(conv, jnp.where(north, 2 - k, k), k)
            spread(conv, jnp.where(south, rows + 5 - k, rows + 3 + k), rows + 3 + k)
        ends(firsts, firsts is not None)
        if firsts is not None:
            def own_step(group, carry):
                rows_of(group, ch)
                return carry

            lax.fori_loop(0, groups, own_step, 0)

    def parcel_copy(group):
        lines = pl.ds(GROUP * group, GROUP)
        return remote(parcel.at[lines], landing.at[lines], parcel_base + group, partner_id)

    def send_rows(group):
        lines = pl.ds(GROUP * group, GROUP)
        parcel[lines] = gradient[pl.ds(1 - ch, 1), lines][0].astype(jnp.bfloat16)
        parcel_copy(group).start()

    def write_smoothed(g, row, columns, value):
        smoothed[g, row, columns] = value

    def write_gradient_one(g, row, columns, value):
        gradient[g, row, columns] = cot[g, row, columns].astype(jnp.float32) + value

    def write_gradient(g, row, columns, value):
        gradient[g, row, columns] = gradient[g, row, columns] + value

    def wide(ref, lines, *lead):
        parts = [
            ref[(*lead, g, lines)].astype(jnp.float32).reshape(GROUP * breadth, lanes)
            for g in range(2)
        ]
        return jnp.concatenate(parts, -1)

    def row_param(index):
        parts = [param[g, 14, index : index + 1] for g in range(2)]
        return jnp.concatenate(parts, -1)

    def store(conv, group, value):
        for g in range(2):
            part = value[:, g * lanes : (g + 1) * lanes].reshape(GROUP, breadth, lanes)
            fields[conv, g, pl.ds(3 + GROUP * group, GROUP)] = part

    def norm_of(group, block):
        value = wide(smoothed, pl.ds(GROUP * group, GROUP)) + row_param(block)
        average = jnp.mean(value, -1, keepdims=True)
        variance = jnp.mean(value * value, -1, keepdims=True) - average * average
        inverse_std = lax.rsqrt(variance + EPSILON)
        normed = (value - average) * inverse_std
        return normed, inverse_std, (normed * row_param(2 + block)).astype(jnp.bfloat16)

    def backward(grad_norm, normed, inverse_std, block):
        grad_scaled = grad_norm.astype(jnp.bfloat16).astype(jnp.float32) * row_param(2 + block)
        first_mean = jnp.mean(grad_scaled, -1, keepdims=True)
        second_mean = jnp.mean(grad_scaled * normed, -1, keepdims=True)
        return (inverse_std * (grad_scaled - first_mean - normed * second_mean)).astype(
            jnp.bfloat16
        )

    def spans():
        return [slice(k * chunk, (k + 1) * chunk) for k in range(2)]

    def first_forward(group):
        normed, inverse_std, scaled = norm_of(group, 0)
        normed_kept[group] = normed
        inverse_kept[group] = inverse_std
        total = None
        for span in spans():
            preact = matmul(scaled, weight_in[0, :, span]) + bias_in[0:1, span]
            value, slope = gelu_parts(preact)
            slope_kept[group, :, span] = slope
            term = matmul(value.astype(jnp.bfloat16), weight_out[0, span])
            total = term if total is None else total + term
        mixed = total.astype(jnp.bfloat16).astype(jnp.float32)
        state = wide(fields, pl.ds(3 + GROUP * group, GROUP), 0)
        store(1, group, (state + row_param(4) * mixed).astype(jnp.bfloat16))

    def second_both(group):
        normed, inverse_std, scaled = norm_of(group, 1)
        grad_mix = (wide(cot, pl.ds(GROUP * group, GROUP)) * row_param(5)).astype(jnp.bfloat16)
        total = None
        for span in spans():
            preact = matmul(scaled, weight_in[1, :, span]) + bias_in[1:2, span]
            slope = gelu_parts(preact)[1]
            grad_act = (matmul_t(grad_mix, weight_out[1, span]) * slope).astype(jnp.bfloat16)
            term = matmul_t(grad_act, weight_in[1, :, span])
            total = term if total is None else total + term
        store(2, group, backward(total, normed, inverse_std, 1))

    def first_backward(group):
        grad_mix = (wide(gradient, pl.ds(GROUP * group, GROUP)) * row_param(4)).astype(
            jnp.bfloat16
        )
        total = None
        for span in spans():
            grad_hidden = matmul_t(grad_mix, weight_out[0, span])
            grad_act = (grad_hidden * slope_kept[group, :, span]).astype(jnp.bfloat16)
            term = matmul_t(grad_act, weight_in[0, :, span])
            total = term if total is None else total + term
        store(3, group, backward(total, normed_kept[group], inverse_kept[group], 0))

    produce(0, lambda group: state_swap(group).wait())
    swaps[0].wait()
    convolve(0, 0, False, write_smoothed)
    produce(1, first_forward)
    convolve(1, 1, False, write_smoothed)
    swaps[1].wait()
    produce(2, second_both)
    convolve(2, 1, True, write_gradient_one)
    produce(3, first_backward)
    convolve(3, 0, True, write_gradient)
    out[pl.ds(ch, 1)] = gradient[pl.ds(ch, 1)]
    for group in range(groups):
        parcel_copy(group).wait()
    out[pl.ds(1 - ch, 1)] = landing[...].astype(jnp.float32)[None]


def local(
    state_field,
    cotangent,
    conv_kernel,
    conv_bias,
    norm_gain,
    weight_in,
    bias_in,
    weight_out,
    layer_scale,
):
    first = lax.axis_index("ch") == 0
    rows, columns, lanes = state_field.shape
    half = columns // 2
    breadth = half + 6
    assert breadth % SPAN == 0 and rows % GROUP == 0 and lax.axis_size("ch") == 2

    def halves(field):
        zero = jnp.zeros((), field.dtype)
        low = field[:, :breadth]
        high = lax.pad(field, zero, ((0, 0, 0), (-half, breadth - half, 0), (0, 0, 0)))
        return jnp.where(first, low, high), jnp.where(first, high, low)

    taps = jnp.pad(conv_kernel, ((0, 0), (0, 0), (0, 1), (0, 0))).reshape(14, 8, lanes)
    rest = jnp.concatenate([conv_bias, norm_gain, layer_scale, layer_scale], 0)[None]
    param = jnp.concatenate([taps, rest], 0)
    groups = rows // GROUP
    hidden = weight_in.shape[2]
    cells = GROUP * breadth
    vmem = pl.BlockSpec(memory_space=pltpu.VMEM)
    result = pl.pallas_call(
        functools.partial(body, half),
        out_shape=jax.ShapeDtypeStruct((2, rows, breadth, lanes), jnp.float32),
        in_specs=[vmem] * 8,
        out_specs=vmem,
        scratch_shapes=[
            pltpu.VMEM((4, 2, rows + 6, breadth, lanes), jnp.bfloat16),
            pltpu.VMEM((2, rows, breadth, lanes), jnp.bfloat16),
            pltpu.VMEM((2, 15, 8, lanes), jnp.float32),
            pltpu.VMEM((4, 2, groups, 2, 16, lanes), jnp.bfloat16),
            pltpu.VMEM((4, 2, groups, 2, 16, lanes), jnp.bfloat16),
            pltpu.VMEM((7, 2, rows + 6, breadth, lanes), jnp.float32),
            pltpu.VMEM((2, rows, breadth, lanes), jnp.float32),
            pltpu.VMEM((groups, cells, 2 * lanes), jnp.float32),
            pltpu.VMEM((groups, cells, 1), jnp.float32),
            pltpu.VMEM((groups, cells, hidden), jnp.float32),
            pltpu.VMEM((2, rows, breadth, lanes), jnp.float32),
            pltpu.VMEM((rows, breadth, lanes), jnp.bfloat16),
            pltpu.VMEM((rows, breadth, lanes), jnp.bfloat16),
            pltpu.SemaphoreType.DMA((10 + 10 * groups,)),
            pltpu.SemaphoreType.DMA((10 + 10 * groups,)),
        ],
        compiler_params=pltpu.CompilerParams(
            collective_id=0, has_side_effects=True, vmem_limit_bytes=60 * 1024 * 1024
        ),
    )(*halves(state_field), *halves(cotangent), param, weight_in, bias_in, weight_out)
    return jnp.concatenate([result[0, :, :half], result[1, :, :half]], 1)


def solution(mesh):
    in_specs = (
        P("lat", "lon", "ch"),
        P("lat", "lon", "ch"),
        P(None, None, None, "ch"),
        P(None, "ch"),
        P(None, "ch"),
        P(),
        P(),
        P(),
        P(None, "ch"),
    )
    out_specs = P("lat", "lon", "ch")
    return jax.shard_map(local, mesh=mesh, in_specs=in_specs, out_specs=out_specs, check_vma=False)
```
